32 devices in a mesh: aux: 4 (over y, x), row: 8 (over z, core).
Axes of the slice: x: 2, y: 2, z: 4, core: 2. Of those that a mesh axis runs over, the one named last changes fastest.
Arguments:
- b_tiles: bfloat16 [4, 8192, 2048], P('aux', 'row'), may hold values from -0.125 to 0.125
- occ_coeff: bfloat16 [8192, 256], P('row'), may hold values from -3 to 3
- tile_blocks: int32 [64, 16], P('row'), may hold values from 0 to 63, as said below
- screen_mask: int32 [64, 16], P('row'), may hold values from 0 to 1, as said below
Outputs:
- exchange: bfloat16 [8192, 8, 4, 256], P('row', None, 'aux')
The draws below stay inside these ranges and needn't reach their ends.
Inputs may be any that keep to these rules, and one draw needn't show every extreme that they name: `tile_blocks`: each entry names a basis block at most 8 blocks away from its own row's block; the first slot of every block names the block itself. `screen_mask`: in every basis block the kept slots come first; some block keeps all 16.
All inputs are finite; a program needn't handle non-finite values.
Results may differ from the reference program's by a relative error of at most 0.0057.
Values may be sent and summed in bfloat16 or wider, within the bound.
A program may use at most 128 MiB of HBM per device.

```python
import jax
import jax.numpy as jnp
from jax import lax

OCC = 256
BS = 128
BLK_DEV = 8
SLOTS = 16
MU_DEV = 1024
NBLK = 64
NBF = 8192
P_TOT = 4
SUB = 256
N_AUX = 4
N_ROW = 8


def draw_tile_blocks(key, part):
    spread_count = 2 * BLK_DEV + 1
    column_index = jnp.arange(spread_count, dtype=jnp.int32)[None, :]
    scores = jax.random.randint(key, (NBLK, spread_count), 0, 2 ** 20) * spread_count + column_index
    scores = jnp.where(column_index == BLK_DEV, -1, scores)
    ranking = jnp.argsort(scores, axis=1, stable=True).astype(jnp.int32)
    offsets = ranking[:, :SLOTS] - BLK_DEV
    anchor = jnp.arange(NBLK, dtype=jnp.int32)[:, None]
    ahead = anchor + offsets
    inside = (ahead >= 0) & (ahead < NBLK)
    return jnp.where(inside, ahead, anchor - offsets).astype(jnp.int32)


def draw_screen_mask(key, part):
    devices = NBLK // BLK_DEV
    key_heavy, key_force, key_high, key_low = jax.random.split(jax.random.fold_in(key, 7), 4)
    heavy = jax.random.randint(key_heavy, (devices,), 0, 4) == 0
    forced = jax.random.randint(key_force, (), 0, devices)
    heavy = heavy | (jnp.arange(devices, dtype=jnp.int32) == forced)
    owners = jnp.arange(NBLK, dtype=jnp.int32) // BLK_DEV
    high = jax.random.randint(key_high, (NBLK,), 12, SLOTS + 1)
    low = jax.random.randint(key_low, (NBLK,), 2, 7)
    counts = jnp.where(heavy[owners], high, low)
    counts = jnp.where(jnp.arange(NBLK, dtype=jnp.int32) == forced * BLK_DEV, SLOTS, counts)
    return (jnp.arange(SLOTS, dtype=jnp.int32)[None, :] < counts[:, None]).astype(jnp.int32)


def block_levels(rng, dims, cuts, smallest, top_value):
    def one(position, shards_of):
        steps = jax.random.uniform(jax.random.fold_in(jax.random.fold_in(rng, 6), position), (shards_of,), jnp.float32, smallest / len(cuts), top_value / len(cuts))
        return jnp.repeat(jnp.exp(steps), dims[position] // shards_of).reshape((-1,) + (1,) * (len(dims) - position - 1))

    loudness = one(*cuts[0])
    for cut in cuts[1:]:
        loudness = loudness * one(*cut)
    return loudness


def gaussian(own_key, extent, spread, limit, cuts=(), kind=jnp.bfloat16):
    values = spread * jax.random.normal(own_key, extent, jnp.float32)
    if cuts:
        values = values * block_levels(own_key, extent, cuts, -0.22, 0.18)
    return jnp.clip(values, -limit, limit).astype(kind)


def setup_inputs(seed: int = 0) -> dict:
    key_of = jax.random.split(jax.random.key(seed), 5)
    b_tiles = gaussian(key_of[0], (P_TOT, NBF, SLOTS * BS), (SLOTS * BS) ** -0.5, 0.125, ((0, 4), (1, 8)))
    occ_coeff = gaussian(key_of[1], (NBF, OCC), 0.5, 3.0, ((0, 8),))
    tile_blocks = draw_tile_blocks(jax.random.fold_in(key_of[4], 71), 0)
    screen_mask = draw_screen_mask(jax.random.fold_in(key_of[4], 71), 0)
    return {"b_tiles": b_tiles, "occ_coeff": occ_coeff, "tile_blocks": tile_blocks, "screen_mask": screen_mask}


def reference(b_tiles, occ_coeff, tile_blocks, screen_mask):
    coeff_blocks = occ_coeff.reshape(NBLK, BS, OCC).astype(jnp.float32)
    tiles = b_tiles.reshape(P_TOT, NBLK, BS, SLOTS, BS)

    def one_block(index):
        block_tiles = lax.dynamic_index_in_dim(tiles, index, 1, keepdims=False).astype(jnp.float32)
        columns = lax.dynamic_index_in_dim(tile_blocks, index, 0, keepdims=False)
        live = lax.dynamic_index_in_dim(screen_mask, index, 0, keepdims=False).astype(jnp.float32)
        picked = coeff_blocks[columns] * live[:, None, None]
        return jnp.einsum("pmsn,sni->pmi", block_tiles, picked, precision=lax.Precision.HIGHEST)

    halves = lax.map(one_block, jnp.arange(NBLK, dtype=jnp.int32)).astype(jnp.bfloat16)
    slab_all = jnp.transpose(halves, (1, 0, 2, 3)).reshape(P_TOT, NBF, OCC).astype(jnp.float32)

    def one_rows(index):
        rows_now = lax.dynamic_slice_in_dim(slab_all, index * MU_DEV, MU_DEV, 1)
        return jnp.einsum("pmi,pli->ml", rows_now, slab_all, precision=lax.Precision.HIGHEST).astype(jnp.bfloat16)

    matrix = lax.map(one_rows, jnp.arange(N_ROW, dtype=jnp.int32))
    return matrix.reshape(NBF, N_ROW, N_AUX, SUB)
```

```python
import functools

import jax
import jax.numpy as jnp
from jax import lax
from jax.experimental import pallas as pl
from jax.experimental.pallas import tpu as pltpu
from jax.sharding import PartitionSpec as P

MESH = pl.DeviceIdType.MESH
VMEM_LIMIT = 48 * 1024 * 1024


def with_halo(block, axis):
    count = lax.axis_size(axis)
    forward = [(i, i + 1) for i in range(count - 1)]
    backward = [(target, source) for source, target in forward]
    low = lax.ppermute(block, axis, forward)
    high = lax.ppermute(block, axis, backward)
    return jnp.concatenate([low, block, high], axis=0)


def half_kernel(slots, size, index_ref, mask_ref, tiles_ref, coeff_ref, half_ref, picked):
    block = pl.program_id(0)
    for slot in range(slots):
        rows = pl.ds(slot * size, size)

        @pl.when(mask_ref[block, slot] != 0)
        def _():
            start = pl.multiple_of(index_ref[block, slot] * size, size)
            picked[rows, :] = coeff_ref[pl.ds(start, size), :]

        @pl.when(mask_ref[block, slot] == 0)
        def _():
            picked[rows, :] = jnp.zeros((size, picked.shape[1]), picked.dtype)

    half_ref[...] = jnp.dot(
        tiles_ref[...], picked[...], preferred_element_type=jnp.float32
    ).astype(half_ref.dtype)


def half_transform(tiles, coeff, index, mask):
    rows, stored = tiles.shape
    blocks, slots = index.shape
    size, orbitals = rows // blocks, coeff.shape[1]
    return pl.pallas_call(
        functools.partial(half_kernel, slots, size),
        out_shape=jax.ShapeDtypeStruct((rows, orbitals), jnp.bfloat16),
        grid_spec=pltpu.PrefetchScalarGridSpec(
            num_scalar_prefetch=2,
            grid=(blocks,),
            in_specs=[
                pl.BlockSpec((size, stored), lambda b, *_: (b, 0)),
                pl.BlockSpec(coeff.shape, lambda b, *_: (0, 0)),
            ],
            out_specs=pl.BlockSpec((size, orbitals), lambda b, *_: (b, 0)),
            scratch_shapes=[pltpu.VMEM((stored, orbitals), jnp.bfloat16)],
        ),
        compiler_params=pltpu.CompilerParams(vmem_limit_bytes=VMEM_LIMIT),
        cost_estimate=pl.CostEstimate(
            flops=2 * rows * stored * orbitals,
            bytes_accessed=2 * rows * stored + 8 * rows * orbitals,
            transcendentals=0,
        ),
    )(index, mask, tiles, coeff)


def exchange_kernel(
    n_aux, n_pos, half_ref, out_ref, slab, part, obuf,
    aux_send, aux_recv, row_send, row_recv, out_sem,
):
    a, r = lax.axis_index("aux"), lax.axis_index("row")
    core, pos = r % 2, r // 2
    sibling = r + 1 - 2 * core
    share = half_ref.shape[1]
    has_up, has_down = pos < n_pos - 1, pos > 0

    barrier = pltpu.get_barrier_semaphore()

    def greet(device):
        pl.semaphore_signal(barrier, inc=1, device_id=device, device_id_type=MESH)

    for j in range(1, n_aux):
        greet(((a + j) % n_aux, r))
    greet((a, sibling))
    pl.when(has_up)(lambda: greet((a, r + 2)))
    pl.when(has_down)(lambda: greet((a, r - 2)))
    ups, downs = (2 * n_pos - 2 - pos) // n_pos, (pos + n_pos - 1) // n_pos
    pl.semaphore_wait(barrier, n_aux + ups + downs)

    def aux_copy(k, j):
        target = (a + j) % n_aux
        quarter = (target + k) % n_aux
        return pltpu.make_async_remote_copy(
            src_ref=half_ref.at[quarter],
            dst_ref=slab.at[j - 1, quarter],
            send_sem=aux_send.at[k, j - 1],
            recv_sem=aux_recv.at[k, j - 1],
            device_id=(target, r),
            device_id_type=MESH,
        )

    def aux_arrival(k, j):
        quarter = (a + k) % n_aux
        return pltpu.make_async_remote_copy(
            src_ref=half_ref.at[quarter],
            dst_ref=slab.at[j - 1, quarter],
            send_sem=aux_send.at[k, j - 1],
            recv_sem=aux_recv.at[k, j - 1],
            device_id=((a + j) % n_aux, r),
            device_id_type=MESH,
        )

    def row_copy(way, origin, j, own=False):
        row = 2 * origin + core
        if not own:
            src = part.at[row, j]
        elif j == 0:
            src = half_ref.at[a]
        else:
            src = slab.at[j - 1, a]
        target = (r + 2, r - 2, sibling)[way]
        return pltpu.make_async_remote_copy(
            src_ref=src,
            dst_ref=part.at[row, j],
            send_sem=row_send.at[way, origin, j],
            recv_sem=row_recv.at[row, j],
            device_id=(a, target),
            device_id_type=MESH,
        )

    def arrival(row, j):
        return pltpu.make_async_remote_copy(
            src_ref=part.at[row, j],
            dst_ref=part.at[row, j],
            send_sem=row_send.at[2, row // 2, j],
            recv_sem=row_recv.at[row, j],
            device_id=(a, sibling),
            device_id_type=MESH,
        )

    def send_own(j):
        pl.when(has_up)(lambda: row_copy(0, pos, j, True).start())
        pl.when(has_down)(lambda: row_copy(1, pos, j, True).start())
        row_copy(2, pos, j, True).start()

    def relay(d, j):
        @pl.when(pos - d >= 0)
        def _():
            origin = pos - d
            arrival(2 * origin + core, j).wait_recv()
            pl.when(has_up)(lambda: row_copy(0, origin, j).start())
            row_copy(2, origin, j).start()

        @pl.when(pos + d < n_pos)
        def _():
            origin = pos + d
            arrival(2 * origin + core, j).wait_recv()
            pl.when(has_down)(lambda: row_copy(1, origin, j).start())
            row_copy(2, origin, j).start()

    def out_copy(row):
        columns = pl.ds(pl.multiple_of(row * share, share), share)
        return pltpu.make_async_copy(obuf.at[row], out_ref.at[:, columns], out_sem.at[row])

    def multiply(row, parts):
        for m in range(n_aux):
            total = None
            for j in range(n_aux):
                left = half_ref[m] if j == 0 else slab[j - 1, m]
                term = lax.dot_general(
                    left, parts(j), (((1,), (1,)), ((), ())),
                    preferred_element_type=jnp.float32,
                )
                total = term if total is None else total + term
            obuf[row, pl.ds(m * share, share), :] = total.astype(obuf.dtype)
        out_copy(row).start()

    def multiply_same(origin):
        row = 2 * origin + core
        multiply(row, lambda j: part[row, j])

    def multiply_other(origin):
        row = 2 * origin + 1 - core
        for j in range(n_aux):
            arrival(row, j).wait_recv()
        multiply(row, lambda j: part[row, j])

    def work(d, which):
        origin = pos - d if which < 2 else pos + d
        live = (origin >= 0) & (origin < n_pos)
        run = multiply_same if which % 2 == 0 else multiply_other
        pl.when(live)(lambda: run(origin))

    for j in range(1, n_aux):
        aux_copy(0, j).start()
    send_own(0)
    for j in range(1, n_aux):
        aux_arrival(0, j).wait_recv()
        send_own(j)
    for k in range(1, n_aux):
        for j in range(1, n_aux):
            aux_copy(k, j).start()
    for j in range(n_aux):
        relay(1, j)
    for k in range(1, n_aux):
        for j in range(1, n_aux):
            aux_arrival(k, j).wait_recv()
    multiply(r, lambda j: half_ref[a] if j == 0 else slab[j - 1, a])
    multiply_other(pos)

    def step(d, carry):
        for j in range(n_aux):
            relay(d, j)
            work(d - 1, j)
        return carry

    lax.fori_loop(2, n_pos, step, 0)
    for which in range(4):
        work(n_pos - 1, which)

    for k in range(n_aux):
        for j in range(1, n_aux):
            aux_copy(k, j).wait_send()
    for j in range(n_aux):
        pl.when(has_up)(lambda: row_copy(0, pos, j, True).wait_send())
        pl.when(has_down)(lambda: row_copy(1, pos, j, True).wait_send())
        row_copy(2, pos, j, True).wait_send()

    def drain(d, carry):
        for j in range(n_aux):
            @pl.when(pos - d >= 0)
            def _():
                pl.when(has_up)(lambda: row_copy(0, pos - d, j).wait_send())
                row_copy(2, pos - d, j).wait_send()

            @pl.when(pos + d < n_pos)
            def _():
                pl.when(has_down)(lambda: row_copy(1, pos + d, j).wait_send())
                row_copy(2, pos + d, j).wait_send()
        return carry

    lax.fori_loop(1, n_pos, drain, 0)

    def finish(row, carry):
        out_copy(row).wait()
        return carry

    lax.fori_loop(0, 2 * n_pos, finish, 0)


def exchange(half, n_aux, n_row):
    rows, orbitals = half.shape
    share, n_pos = rows // n_aux, n_row // 2
    return pl.pallas_call(
        functools.partial(exchange_kernel, n_aux, n_pos),
        out_shape=jax.ShapeDtypeStruct((rows, n_row * share), jnp.bfloat16),
        in_specs=[pl.BlockSpec(memory_space=pltpu.VMEM)],
        out_specs=pl.BlockSpec(memory_space=pl.ANY),
        scratch_shapes=[
            pltpu.VMEM((n_aux - 1, n_aux, share, orbitals), jnp.bfloat16),
            pltpu.VMEM((n_row, n_aux, share, orbitals), jnp.bfloat16),
            pltpu.VMEM((n_row, rows, share), jnp.bfloat16),
            pltpu.SemaphoreType.DMA((n_aux, n_aux - 1)),
            pltpu.SemaphoreType.DMA((n_aux, n_aux - 1)),
            pltpu.SemaphoreType.DMA((3, n_pos, n_aux)),
            pltpu.SemaphoreType.DMA((n_row, n_aux)),
            pltpu.SemaphoreType.DMA((n_row,)),
        ],
        compiler_params=pltpu.CompilerParams(
            collective_id=0, has_side_effects=True, vmem_limit_bytes=VMEM_LIMIT
        ),
        cost_estimate=pl.CostEstimate(
            flops=2 * rows * rows * n_row * share,
            bytes_accessed=2 * rows * n_row * share,
            transcendentals=0,
        ),
    )(half.reshape(n_aux, share, orbitals))


def per_device(b_tiles, occ_coeff, tile_blocks, screen_mask):
    rows = b_tiles.shape[1]
    blocks = tile_blocks.shape[0]
    n_aux, n_row = lax.axis_size("aux"), lax.axis_size("row")
    extended = with_halo(occ_coeff, "row")
    index = tile_blocks - (lax.axis_index("row") - 1) * blocks
    half = half_transform(b_tiles[0], extended, index, screen_mask)
    result = exchange(half, n_aux, n_row)
    return result.reshape(rows, n_row, 1, rows // n_aux)


def solution(mesh):
    in_specs = (P("aux", "row", None), P("row", None), P("row", None), P("row", None))
    out_specs = P("row", None, "aux", None)
    return jax.shard_map(
        per_device, mesh=mesh, in_specs=in_specs, out_specs=out_specs, check_vma=False
    )
```

```python
import functools

import jax
import jax.numpy as jnp
from jax import lax
from jax.experimental import pallas as pl
from jax.experimental.pallas import tpu as pltpu
from jax.sharding import PartitionSpec as P

MESH = pl.DeviceIdType.MESH
VMEM_LIMIT = 48 * 1024 * 1024


def with_halo(block, axis):
    count = lax.axis_size(axis)
    forward = [(i, i + 1) for i in range(count - 1)]
    backward = [(target, source) for source, target in forward]
    low = lax.ppermute(block, axis, forward)
    high = lax.ppermute(block, axis, backward)
    return jnp.concatenate([low, block, high], axis=0)


def half_kernel(slots, size, index_ref, mask_ref, tiles_ref, coeff_ref, half_ref, picked):
    block = pl.program_id(0)
    for slot in range(slots):
        rows = pl.ds(slot * size, size)

        @pl.when(mask_ref[block, slot] != 0)
        def _():
            start = pl.multiple_of(index_ref[block, slot] * size, size)
            picked[rows, :] = coeff_ref[pl.ds(start, size), :]

        @pl.when(mask_ref[block, slot] == 0)
        def _():
            picked[rows, :] = jnp.zeros((size, picked.shape[1]), picked.dtype)

    half_ref[...] = jnp.dot(
        tiles_ref[...], picked[...], preferred_element_type=jnp.float32
    ).astype(half_ref.dtype)


def half_transform(tiles, coeff, index, mask):
    rows, stored = tiles.shape
    blocks, slots = index.shape
    size, orbitals = rows // blocks, coeff.shape[1]
    return pl.pallas_call(
        functools.partial(half_kernel, slots, size),
        out_shape=jax.ShapeDtypeStruct((rows, orbitals), jnp.bfloat16),
        grid_spec=pltpu.PrefetchScalarGridSpec(
            num_scalar_prefetch=2,
            grid=(blocks,),
            in_specs=[
                pl.BlockSpec((size, stored), lambda b, *_: (b, 0)),
                pl.BlockSpec(coeff.shape, lambda b, *_: (0, 0)),
            ],
            out_specs=pl.BlockSpec((size, orbitals), lambda b, *_: (b, 0)),
            scratch_shapes=[pltpu.VMEM((stored, orbitals), jnp.bfloat16)],
        ),
        compiler_params=pltpu.CompilerParams(vmem_limit_bytes=VMEM_LIMIT),
        cost_estimate=pl.CostEstimate(
            flops=2 * rows * stored * orbitals,
            bytes_accessed=2 * rows * stored + 8 * rows * orbitals,
            transcendentals=0,
        ),
    )(index, mask, tiles, coeff)


def exchange_kernel(
    n_aux, n_pos, half_ref, out_ref, slab, part, obuf,
    aux_send, aux_recv, row_send, row_recv, out_sem,
):
    a, r = lax.axis_index("aux"), lax.axis_index("row")
    core, pos = r % 2, r // 2
    sibling = r + 1 - 2 * core
    share = half_ref.shape[1]
    has_up, has_down = pos < n_pos - 1, pos > 0

    barrier = pltpu.get_barrier_semaphore()

    def greet(device):
        pl.semaphore_signal(barrier, inc=1, device_id=device, device_id_type=MESH)

    for j in range(1, n_aux):
        greet(((a + j) % n_aux, r))
    greet((a, sibling))
    pl.when(has_up)(lambda: greet((a, r + 2)))
    pl.when(has_down)(lambda: greet((a, r - 2)))
    ups, downs = (2 * n_pos - 2 - pos) // n_pos, (pos + n_pos - 1) // n_pos
    pl.semaphore_wait(barrier, n_aux + ups + downs)

    def aux_copy(k, j):
        target = (a + j) % n_aux
        quarter = (target + k) % n_aux
        return pltpu.make_async_remote_copy(
            src_ref=half_ref.at[quarter],
            dst_ref=slab.at[j - 1, quarter],
            send_sem=aux_send.at[k, j - 1],
            recv_sem=aux_recv.at[k, j - 1],
            device_id=(target, r),
            device_id_type=MESH,
        )

    def aux_arrival(k, j):
        quarter = (a + k) % n_aux
        return pltpu.make_async_remote_copy(
            src_ref=half_ref.at[quarter],
            dst_ref=slab.at[j - 1, quarter],
            send_sem=aux_send.at[k, j - 1],
            recv_sem=aux_recv.at[k, j - 1],
            device_id=((a + j) % n_aux, r),
            device_id_type=MESH,
        )

    def row_copy(way, origin, j, own=False):
        row = 2 * origin + core
        if not own:
            src = part.at[row, j]
        elif j == 0:
            src = half_ref.at[a]
        else:
            src = slab.at[j - 1, a]
        target = (r + 2, r - 2, sibling)[way]
        return pltpu.make_async_remote_copy(
            src_ref=src,
            dst_ref=part.at[row, j],
            send_sem=row_send.at[way, origin, j],
            recv_sem=row_recv.at[row, j],
            device_id=(a, target),
            device_id_type=MESH,
        )

    def arrival(row, j):
        return pltpu.make_async_remote_copy(
            src_ref=part.at[row, j],
            dst_ref=part.at[row, j],
            send_sem=row_send.at[2, row // 2, j],
            recv_sem=row_recv.at[row, j],
            device_id=(a, sibling),
            device_id_type=MESH,
        )

    def send_own(j):
        pl.when(has_up)(lambda: row_copy(0, pos, j, True).start())
        pl.when(has_down)(lambda: row_copy(1, pos, j, True).start())
        row_copy(2, pos, j, True).start()

    def relay(d, j):
        @pl.when(pos - d >= 0)
        def _():
            origin = pos - d
            arrival(2 * origin + core, j).wait_recv()
            pl.when(has_up)(lambda: row_copy(0, origin, j).start())
            row_copy(2, origin, j).start()

        @pl.when(pos + d < n_pos)
        def _():
            origin = pos + d
            arrival(2 * origin + core, j).wait_recv()
            pl.when(has_down)(lambda: row_copy(1, origin, j).start())
            row_copy(2, origin, j).start()

    def out_copy(row):
        columns = pl.ds(pl.multiple_of(row * share, share), share)
        return pltpu.make_async_copy(obuf.at[row], out_ref.at[:, columns], out_sem.at[row])

    def multiply(row, parts):
        for m in range(n_aux):
            total = None
            for j in range(n_aux):
                left = half_ref[m] if j == 0 else slab[j - 1, m]
                term = lax.dot_general(
                    left, parts(j), (((1,), (1,)), ((), ())),
                    preferred_element_type=jnp.float32,
                )
                total = term if total is None else total + term
            obuf[row, pl.ds(m * share, share), :] = total.astype(obuf.dtype)
        out_copy(row).start()

    def multiply_same(origin):
        row = 2 * origin + core
        multiply(row, lambda j: part[row, j])

    def multiply_other(origin):
        row = 2 * origin + 1 - core
        for j in range(n_aux):
            arrival(row, j).wait_recv()
        multiply(row, lambda j: part[row, j])

    def work(d, which):
        origin = pos - d if which < 2 else pos + d
        live = (origin >= 0) & (origin < n_pos)
        run = multiply_same if which % 2 == 0 else multiply_other
        pl.when(live)(lambda: run(origin))

    for j in range(1, n_aux):
        aux_copy(0, j).start()
    send_own(0)
    for j in range(1, n_aux):
        aux_arrival(0, j).wait_recv()
        send_own(j)
    for k in range(1, n_aux):
        for j in range(1, n_aux):
            aux_copy(k, j).start()
    for d in (1, 2):
        for j in range(n_aux):
            relay(d, j)
    for k in range(1, n_aux):
        for j in range(1, n_aux):
            aux_arrival(k, j).wait_recv()
    multiply(r, lambda j: half_ref[a] if j == 0 else slab[j - 1, a])
    multiply_other(pos)
    for which in range(4):
        work(1, which)

    def step(d, carry):
        for j in range(n_aux):
            relay(d, j)
            work(d - 1, j)
        return carry

    lax.fori_loop(3, n_pos, step, 0)
    for which in range(4):
        work(n_pos - 1, which)

    for k in range(n_aux):
        for j in range(1, n_aux):
            aux_copy(k, j).wait_send()
    for j in range(n_aux):
        pl.when(has_up)(lambda: row_copy(0, pos, j, True).wait_send())
        pl.when(has_down)(lambda: row_copy(1, pos, j, True).wait_send())
        row_copy(2, pos, j, True).wait_send()

    def drain(d, carry):
        for j in range(n_aux):
            @pl.when(pos - d >= 0)
            def _():
                pl.when(has_up)(lambda: row_copy(0, pos - d, j).wait_send())
                row_copy(2, pos - d, j).wait_send()

            @pl.when(pos + d < n_pos)
            def _():
                pl.when(has_down)(lambda: row_copy(1, pos + d, j).wait_send())
                row_copy(2, pos + d, j).wait_send()
        return carry

    lax.fori_loop(1, n_pos, drain, 0)

    def finish(row, carry):
        out_copy(row).wait()
        return carry

    lax.fori_loop(0, 2 * n_pos, finish, 0)


def exchange(half, n_aux, n_row):
    rows, orbitals = half.shape
    share, n_pos = rows // n_aux, n_row // 2
    return pl.pallas_call(
        functools.partial(exchange_kernel, n_aux, n_pos),
        out_shape=jax.ShapeDtypeStruct((rows, n_row * share), jnp.bfloat16),
        in_specs=[pl.BlockSpec(memory_space=pltpu.VMEM)],
        out_specs=pl.BlockSpec(memory_space=pl.ANY),
        scratch_shapes=[
            pltpu.VMEM((n_aux - 1, n_aux, share, orbitals), jnp.bfloat16),
            pltpu.VMEM((n_row, n_aux, share, orbitals), jnp.bfloat16),
            pltpu.VMEM((n_row, rows, share), jnp.bfloat16),
            pltpu.SemaphoreType.DMA((n_aux, n_aux - 1)),
            pltpu.SemaphoreType.DMA((n_aux, n_aux - 1)),
            pltpu.SemaphoreType.DMA((3, n_pos, n_aux)),
            pltpu.SemaphoreType.DMA((n_row, n_aux)),
            pltpu.SemaphoreType.DMA((n_row,)),
        ],
        compiler_params=pltpu.CompilerParams(
            collective_id=0, has_side_effects=True, vmem_limit_bytes=VMEM_LIMIT
        ),
        cost_estimate=pl.CostEstimate(
            flops=2 * rows * rows * n_row * share,
            bytes_accessed=2 * rows * n_row * share,
            transcendentals=0,
        ),
    )(half.reshape(n_aux, share, orbitals))


def per_device(b_tiles, occ_coeff, tile_blocks, screen_mask):
    rows = b_tiles.shape[1]
    blocks = tile_blocks.shape[0]
    n_aux, n_row = lax.axis_size("aux"), lax.axis_size("row")
    extended = with_halo(occ_coeff, "row")
    index = tile_blocks - (lax.axis_index("row") - 1) * blocks
    half = half_transform(b_tiles[0], extended, index, screen_mask)
    result = exchange(half, n_aux, n_row)
    return result.reshape(rows, n_row, 1, rows // n_aux)


def solution(mesh):
    in_specs = (P("aux", "row", None), P("row", None), P("row", None), P("row", None))
    out_specs = P("row", None, "aux", None)
    return jax.shard_map(
        per_device, mesh=mesh, in_specs=in_specs, out_specs=out_specs, check_vma=False
    )
```

```python
import functools

import jax
import jax.numpy as jnp
from jax import lax
from jax.experimental import pallas as pl
from jax.experimental.pallas import tpu as pltpu
from jax.sharding import PartitionSpec as P

MESH = pl.DeviceIdType.MESH
VMEM_LIMIT = 48 * 1024 * 1024


def with_halo(block, axis):
    count = lax.axis_size(axis)
    forward = [(i, i + 1) for i in range(count - 1)]
    backward = [(target, source) for source, target in forward]
    low = lax.ppermute(block, axis, forward)
    high = lax.ppermute(block, axis, backward)
    return jnp.concatenate([low, block, high], axis=0)


def half_kernel(slots, size, index_ref, mask_ref, tiles_ref, coeff_ref, half_ref):
    block = pl.program_id(0)

    def picked(slot):
        start = pl.multiple_of(index_ref[block, slot] * size, size)
        rows = coeff_ref[pl.ds(start, size), :]
        return jnp.where(mask_ref[block, slot] != 0, rows, jnp.zeros_like(rows))

    total = None
    for slot in range(0, slots, 2):
        pair = jnp.concatenate([picked(slot), picked(slot + 1)], axis=0)
        term = jnp.dot(
            tiles_ref[:, slot * size:(slot + 2) * size], pair,
            preferred_element_type=jnp.float32,
        )
        total = term if total is None else total + term
    half_ref[...] = total.astype(half_ref.dtype)


def half_transform(tiles, coeff, index, mask):
    rows, stored = tiles.shape
    blocks, slots = index.shape
    size, orbitals = rows // blocks, coeff.shape[1]
    return pl.pallas_call(
        functools.partial(half_kernel, slots, size),
        out_shape=jax.ShapeDtypeStruct((rows, orbitals), jnp.bfloat16),
        grid_spec=pltpu.PrefetchScalarGridSpec(
            num_scalar_prefetch=2,
            grid=(blocks,),
            in_specs=[
                pl.BlockSpec((size, stored), lambda b, *_: (b, 0)),
                pl.BlockSpec(coeff.shape, lambda b, *_: (0, 0)),
            ],
            out_specs=pl.BlockSpec((size, orbitals), lambda b, *_: (b, 0)),
        ),
        compiler_params=pltpu.CompilerParams(vmem_limit_bytes=VMEM_LIMIT),
        cost_estimate=pl.CostEstimate(
            flops=2 * rows * stored * orbitals,
            bytes_accessed=2 * rows * stored + 8 * rows * orbitals,
            transcendentals=0,
        ),
    )(index, mask, tiles, coeff)


def exchange_kernel(
    n_aux, n_pos, half_ref, out_ref, slab, part, obuf,
    aux_send, aux_recv, row_send, row_recv, out_sem,
):
    a, r = lax.axis_index("aux"), lax.axis_index("row")
    core, pos = r % 2, r // 2
    sibling = r + 1 - 2 * core
    share = half_ref.shape[1]
    has_up, has_down = pos < n_pos - 1, pos > 0

    barrier = pltpu.get_barrier_semaphore()

    def greet(device):
        pl.semaphore_signal(barrier, inc=1, device_id=device, device_id_type=MESH)

    for j in range(1, n_aux):
        greet(((a + j) % n_aux, r))
    greet((a, sibling))
    pl.when(has_up)(lambda: greet((a, r + 2)))
    pl.when(has_down)(lambda: greet((a, r - 2)))
    ups, downs = (2 * n_pos - 2 - pos) // n_pos, (pos + n_pos - 1) // n_pos
    pl.semaphore_wait(barrier, n_aux + ups + downs)

    def aux_copy(k, j):
        target = (a + j) % n_aux
        quarter = (target + k) % n_aux
        return pltpu.make_async_remote_copy(
            src_ref=half_ref.at[quarter],
            dst_ref=slab.at[j - 1, quarter],
            send_sem=aux_send.at[k, j - 1],
            recv_sem=aux_recv.at[k, j - 1],
            device_id=(target, r),
            device_id_type=MESH,
        )

    def aux_arrival(k, j):
        quarter = (a + k) % n_aux
        return pltpu.make_async_remote_copy(
            src_ref=half_ref.at[quarter],
            dst_ref=slab.at[j - 1, quarter],
            send_sem=aux_send.at[k, j - 1],
            recv_sem=aux_recv.at[k, j - 1],
            device_id=((a + j) % n_aux, r),
            device_id_type=MESH,
        )

    def row_copy(way, origin, j, own=False):
        row = 2 * origin + core
        if not own:
            src = part.at[row, j]
        elif j == 0:
            src = half_ref.at[a]
        else:
            src = slab.at[j - 1, a]
        target = (r + 2, r - 2, sibling)[way]
        return pltpu.make_async_remote_copy(
            src_ref=src,
            dst_ref=part.at[row, j],
            send_sem=row_send.at[way, origin, j],
            recv_sem=row_recv.at[row, j],
            device_id=(a, target),
            device_id_type=MESH,
        )

    def arrival(row, j):
        return pltpu.make_async_remote_copy(
            src_ref=part.at[row, j],
            dst_ref=part.at[row, j],
            send_sem=row_send.at[2, row // 2, j],
            recv_sem=row_recv.at[row, j],
            device_id=(a, sibling),
            device_id_type=MESH,
        )

    def send_own(j):
        pl.when(has_up)(lambda: row_copy(0, pos, j, True).start())
        pl.when(has_down)(lambda: row_copy(1, pos, j, True).start())
        row_copy(2, pos, j, True).start()

    def relay(d, j):
        @pl.when(pos - d >= 0)
        def _():
            origin = pos - d
            arrival(2 * origin + core, j).wait_recv()
            pl.when(has_up)(lambda: row_copy(0, origin, j).start())
            row_copy(2, origin, j).start()

        @pl.when(pos + d < n_pos)
        def _():
            origin = pos + d
            arrival(2 * origin + core, j).wait_recv()
            pl.when(has_down)(lambda: row_copy(1, origin, j).start())
            row_copy(2, origin, j).start()

    def out_copy(row):
        columns = pl.ds(pl.multiple_of(row * share, share), share)
        return pltpu.make_async_copy(obuf.at[row], out_ref.at[:, columns], out_sem.at[row])

    def multiply(row, parts):
        for m in range(n_aux):
            total = None
            for j in range(n_aux):
                left = half_ref[m] if j == 0 else slab[j - 1, m]
                term = lax.dot_general(
                    left, parts(j), (((1,), (1,)), ((), ())),
                    preferred_element_type=jnp.float32,
                )
                total = term if total is None else total + term
            obuf[row, pl.ds(m * share, share), :] = total.astype(obuf.dtype)
        out_copy(row).start()

    def multiply_same(origin):
        row = 2 * origin + core
        multiply(row, lambda j: part[row, j])

    def multiply_other(origin):
        row = 2 * origin + 1 - core
        for j in range(n_aux):
            arrival(row, j).wait_recv()
        multiply(row, lambda j: part[row, j])

    def work(d, which):
        origin = pos - d if which < 2 else pos + d
        live = (origin >= 0) & (origin < n_pos)
        run = multiply_same if which % 2 == 0 else multiply_other
        pl.when(live)(lambda: run(origin))

    for j in range(1, n_aux):
        aux_copy(0, j).start()
    send_own(0)
    for j in range(1, n_aux):
        aux_arrival(0, j).wait_recv()
        send_own(j)
    for k in range(1, n_aux):
        for j in range(1, n_aux):
            aux_copy(k, j).start()
    for d in (1, 2):
        for j in range(n_aux):
            relay(d, j)
    for k in range(1, n_aux):
        for j in range(1, n_aux):
            aux_arrival(k, j).wait_recv()
    multiply(r, lambda j: half_ref[a] if j == 0 else slab[j - 1, a])
    multiply_other(pos)
    for which in range(4):
        work(1, which)

    def step(d, carry):
        for j in range(n_aux):
            relay(d, j)
            work(d - 1, j)
        return carry

    lax.fori_loop(3, n_pos, step, 0)
    for which in range(4):
        work(n_pos - 1, which)

    for k in range(n_aux):
        for j in range(1, n_aux):
            aux_copy(k, j).wait_send()
    for j in range(n_aux):
        pl.when(has_up)(lambda: row_copy(0, pos, j, True).wait_send())
        pl.when(has_down)(lambda: row_copy(1, pos, j, True).wait_send())
        row_copy(2, pos, j, True).wait_send()

    def drain(d, carry):
        for j in range(n_aux):
            @pl.when(pos - d >= 0)
            def _():
                pl.when(has_up)(lambda: row_copy(0, pos - d, j).wait_send())
                row_copy(2, pos - d, j).wait_send()

            @pl.when(pos + d < n_pos)
            def _():
                pl.when(has_down)(lambda: row_copy(1, pos + d, j).wait_send())
                row_copy(2, pos + d, j).wait_send()
        return carry

    lax.fori_loop(1, n_pos, drain, 0)

    def finish(row, carry):
        out_copy(row).wait()
        return carry

    lax.fori_loop(0, 2 * n_pos, finish, 0)


def exchange(half, n_aux, n_row):
    rows, orbitals = half.shape
    share, n_pos = rows // n_aux, n_row // 2
    return pl.pallas_call(
        functools.partial(exchange_kernel, n_aux, n_pos),
        out_shape=jax.ShapeDtypeStruct((rows, n_row * share), jnp.bfloat16),
        in_specs=[pl.BlockSpec(memory_space=pltpu.VMEM)],
        out_specs=pl.BlockSpec(memory_space=pl.ANY),
        scratch_shapes=[
            pltpu.VMEM((n_aux - 1, n_aux, share, orbitals), jnp.bfloat16),
            pltpu.VMEM((n_row, n_aux, share, orbitals), jnp.bfloat16),
            pltpu.VMEM((n_row, rows, share), jnp.bfloat16),
            pltpu.SemaphoreType.DMA((n_aux, n_aux - 1)),
            pltpu.SemaphoreType.DMA((n_aux, n_aux - 1)),
            pltpu.SemaphoreType.DMA((3, n_pos, n_aux)),
            pltpu.SemaphoreType.DMA((n_row, n_aux)),
            pltpu.SemaphoreType.DMA((n_row,)),
        ],
        compiler_params=pltpu.CompilerParams(
            collective_id=0, has_side_effects=True, vmem_limit_bytes=VMEM_LIMIT
        ),
        cost_estimate=pl.CostEstimate(
            flops=2 * rows * rows * n_row * share,
            bytes_accessed=2 * rows * n_row * share,
            transcendentals=0,
        ),
    )(half.reshape(n_aux, share, orbitals))


def per_device(b_tiles, occ_coeff, tile_blocks, screen_mask):
    rows = b_tiles.shape[1]
    blocks = tile_blocks.shape[0]
    n_aux, n_row = lax.axis_size("aux"), lax.axis_size("row")
    extended = with_halo(occ_coeff, "row")
    index = tile_blocks - (lax.axis_index("row") - 1) * blocks
    half = half_transform(b_tiles[0], extended, index, screen_mask)
    result = exchange(half, n_aux, n_row)
    return result.reshape(rows, n_row, 1, rows // n_aux)


def solution(mesh):
    in_specs = (P("aux", "row", None), P("row", None), P("row", None), P("row", None))
    out_specs = P("row", None, "aux", None)
    return jax.shard_map(
        per_device, mesh=mesh, in_specs=in_specs, out_specs=out_specs, check_vma=False
    )
```
